32 devices in a mesh: groups: 2 (over x), tm: 16 (over z, y, core).
Axes of the slice: x: 2, y: 2, z: 4, core: 2. Of those that a mesh axis runs over, the one named last changes fastest.
Arguments:
- hyper: float32 [6], P('groups'), parts along dimension 0, may hold values from 0.5 to 0.9
- spatial_prec: float32 [768, 768], replicated, as said below
- part_lengths: int32 [32], P('groups'), parts along dimension 0, may hold values from 1 to 2, as said below
- reading_index: int32 [4, 32, 1024], P(None, ('groups', 'tm')), parts along dimension 1, may hold values from 0 to 767, as said below
- reading_value: float32 [4, 32, 1024], P(None, ('groups', 'tm')), parts along dimension 1, as said below
- reading_cov: float32 [16, 32, 1024], P(None, ('groups', 'tm')), parts along dimension 1, may hold values from -0.1875 to 0.1875
Outputs:
- sep_block: float32 [32, 768, 768], P(('groups', 'tm')), parts along dimension 0
- fill_block: float32 [32, 768, 768], P(('groups', 'tm')), parts along dimension 0
- sep_border: float32 [32, 16, 768], P(('groups', 'tm')), parts along dimension 0
- tip: float32 [32, 16], P('groups'), parts along dimension 0
The draws below stay inside these ranges and needn't reach their ends.
There are 2 independent parts, one for each index of `groups`. The reference program is written for one: setup_inputs(seed, part) draws one part's arguments, and reference() takes and returns one part's arrays. A program takes and returns all parts, laid end to end along the dimension named above; an argument that names none is the same for every part. Nothing has to cross between parts.
Inputs may be any that keep to these rules, and one draw needn't show every extreme that they name: `reading_index`: row 0 is a reading's day, rows 1 to 3 the mesh nodes of its triangle's vertices. On every device, column block k (columns k * 64 to (k + 1) * 64 - 1) holds readings whose day lies in time partition k. `part_lengths`: partition k holds the days that follow those of partitions 0 to k - 1; exactly 8 partitions hold 2 days, the others 1. `reading_value`: row 0 is the linear predictor; rows 1 to 3 are positive barycentric weights summing to 1 for each reading. `spatial_prec`: A symmetric sparse mesh precision: each row has a few nonpositive neighbour entries, and a positive diagonal that exceeds the sum of magnitudes of its row's other entries.
All inputs are finite; a program needn't handle non-finite values.
Results may differ from the reference program's by a relative error of at most 0.0003.
Values sent between devices are 32-bit elements; how exact they have to be, the bound alone decides.
A program may use at most 128 MiB of HBM per device.

```python
import jax
import jax.numpy as jnp
from jax import lax

M = 768
P_SIZE = 16
CAP = 64
READ_DEV = 1024
N_TM = 16


def partition_lengths(key):
    ranking = jax.random.permutation(jax.random.fold_in(key, 11), N_TM)
    return (1 + (ranking < N_TM // 2).astype(jnp.int32)).astype(jnp.int32)


def draw_part_lengths(key, part):
    return partition_lengths(key)


def draw_reading_index(key, part):
    lengths = partition_lengths(key)
    part_ends = (jnp.cumsum(lengths) - 1).astype(jnp.int32)
    bucket = jnp.arange(N_TM * CAP, dtype=jnp.int32) // CAP
    step_back = jax.random.randint(jax.random.fold_in(key, 12), (N_TM, N_TM * CAP), 0, 2).astype(jnp.int32)
    day_ids = part_ends[bucket][None, :] - step_back * (lengths[bucket][None, :] - 1)
    vertex_ids = jax.random.randint(jax.random.fold_in(key, 13), (3, N_TM, N_TM * CAP), 0, M).astype(jnp.int32)
    return jnp.concatenate([day_ids[None].astype(jnp.int32), vertex_ids], axis=0)


def draw_reading_value(key, part):
    first_key = jax.random.fold_in(key, 21)
    second_key = jax.random.fold_in(key, 22)
    linear = jnp.clip(0.5 * jax.random.normal(first_key, (N_TM, N_TM * CAP)), -1.5, 1.5)
    uniform_draws = jax.random.uniform(second_key, (3, N_TM, N_TM * CAP), minval=0.2, maxval=1.0)
    bary_weights = uniform_draws / jnp.sum(uniform_draws, axis=0, keepdims=True)
    return jnp.concatenate([linear[None], bary_weights], axis=0).astype(jnp.float32)


def draw_spatial_prec(key, part):
    offsets = [1, 2, 3, 5, 8, 13]
    rows = jnp.arange(M, dtype=jnp.int32)[:, None]
    cols = jnp.arange(M, dtype=jnp.int32)[None, :]
    distance = (cols - rows) % M
    magnitudes = jax.random.uniform(jax.random.fold_in(key, 31), (M, len(offsets)), minval=0.5, maxval=1.5)
    upper = jnp.zeros((M, M), jnp.float32)
    for index in range(len(offsets)):
        upper = upper + jnp.where(distance == offsets[index], magnitudes[:, index:index + 1], 0.0)
    neighbours = 0.125 * (upper + upper.T)
    row_total = jnp.sum(neighbours, axis=1)
    ratio = jax.random.uniform(jax.random.fold_in(key, 32), (M,), minval=0.5, maxval=0.9)
    identity = jnp.eye(M, dtype=jnp.float32)
    return (identity * (row_total / ratio)[None, :] - neighbours).astype(jnp.float32)


def block_scale(key, dims, split, least, high):
    loudness, own = 1.0, jax.random.fold_in(key, 6)
    for dim, parts in split:
        steps = jnp.exp(jax.random.uniform(jax.random.fold_in(own, dim), (parts,), jnp.float32, least / len(split), high / len(split)))
        loudness = loudness * jnp.repeat(steps, dims[dim] // parts).reshape([-1 if axis == dim else 1 for axis in range(len(dims))])
    return loudness


def scatter_about(key, extent, spread, reach, shards=(), kind=jnp.bfloat16):
    factor_of = block_scale(key, extent, shards, -0.22, 0.18) if shards else 1.0
    values = jax.random.normal(key, extent, jnp.float32) * spread * factor_of
    return jnp.minimum(jnp.maximum(values, -reach), reach).astype(kind)


def setup_inputs(seed: int = 0, part: int = 0) -> dict:
    key_of = jax.random.split(jax.random.key(seed), 7)
    part_splits = jax.random.split(jax.random.fold_in(key_of[6], part), 7)
    hyper = jnp.clip(jax.random.uniform(part_splits[0], (3,), jnp.float32, 0.5, 0.9), 0.5, 0.9)
    spatial_prec = draw_spatial_prec(jax.random.fold_in(key_of[6], 71), part)
    part_lengths = draw_part_lengths(jax.random.fold_in(jax.random.fold_in(key_of[6], part), 71), part)
    reading_index = draw_reading_index(jax.random.fold_in(jax.random.fold_in(key_of[6], part), 71), part)
    reading_value = draw_reading_value(jax.random.fold_in(jax.random.fold_in(key_of[6], part), 71), part)
    reading_cov = scatter_about(part_splits[5], (P_SIZE, N_TM, N_TM * CAP), READ_DEV ** -0.5, 0.1875, ((1, 16),), jnp.float32)
    return {"hyper": hyper, "spatial_prec": spatial_prec, "part_lengths": part_lengths, "reading_index": reading_index, "reading_value": reading_value, "reading_cov": reading_cov}


HIGHEST = lax.Precision.HIGHEST

def assemble(records_int, records_float, covariate, my_end, mesh_width):
    total_reads = records_int.shape[1] * records_int.shape[2]
    records_int = records_int.reshape(4, total_reads)
    records_float = records_float.reshape(4, total_reads)
    covariate = covariate.reshape(covariate.shape[0], total_reads)
    day_slot = (my_end - records_int[0]).astype(jnp.int32)
    weight = jnp.exp(records_float[0])
    vertex_ids = records_int[1:4]
    bary_weights = records_float[1:4]
    scaled = bary_weights * weight[None, :]
    block_start = day_slot * (mesh_width * mesh_width)
    positions = (block_start[None, None, :] + vertex_ids[:, None, :] * mesh_width + vertex_ids[None, :, :]).reshape(-1)
    entries = (scaled[:, None, :] * bary_weights[None, :, :]).reshape(-1)
    hessian = jnp.zeros((2 * mesh_width * mesh_width,), jnp.float32).at[positions].add(entries)
    hessian = hessian.reshape(2, mesh_width, mesh_width)
    border_rows = (day_slot[None, :] * mesh_width + vertex_ids).reshape(-1)
    border_terms = (covariate[:, None, :] * scaled[None, :, :]).reshape(covariate.shape[0], -1)
    border = jnp.zeros((covariate.shape[0], 2 * mesh_width), jnp.float32).at[:, border_rows].add(border_terms)
    border = border.reshape(covariate.shape[0], 2, mesh_width).transpose(1, 0, 2)
    tip_data = jnp.dot(covariate * weight[None, :], covariate.T, precision=HIGHEST)
    return (hessian, border, tip_data)

def eliminate(hessian, border, prior_diag, coupling_block):
    mesh_width = coupling_block.shape[0]
    interior = hessian[1] + prior_diag
    factor = jnp.linalg.cholesky(interior)
    stacked = jnp.concatenate([coupling_block, border[1].T], axis=1)
    solved = jax.scipy.linalg.solve_triangular(factor, stacked, lower=True)
    across = solved[:, :mesh_width]
    toward = solved[:, mesh_width:]
    schur_update = -jnp.dot(across.T, across, precision=HIGHEST)
    lateral_block = -jnp.dot(toward.T, across, precision=HIGHEST)
    apex_schur_block = -jnp.dot(toward.T, toward, precision=HIGHEST)
    return (schur_update, lateral_block, apex_schur_block)

def reference(hyper, spatial_prec, part_lengths, reading_index, reading_value, reading_cov):
    mesh_width = spatial_prec.shape[0]
    covars = reading_cov.shape[0]
    corr_time = hyper[0]
    tau_field = hyper[1]
    tau_fixed = hyper[2]
    prior_diag = (1.0 + corr_time * corr_time) * tau_field * spatial_prec
    coupling_block = -corr_time * tau_field * spatial_prec
    part_ends = (jnp.cumsum(part_lengths) - 1).astype(jnp.int32)

    def one_part(partition_position):
        start_col = (partition_position * CAP).astype(jnp.int32)
        records_int = lax.dynamic_slice_in_dim(reading_index, start_col, CAP, 2)
        records_float = lax.dynamic_slice_in_dim(reading_value, start_col, CAP, 2)
        covariate = lax.dynamic_slice_in_dim(reading_cov, start_col, CAP, 2)
        my_end = part_ends[partition_position]
        local_length = part_lengths[partition_position]
        hessian, border, tip_data = assemble(records_int, records_float, covariate, my_end, mesh_width)

        def perform_elimination():
            return eliminate(hessian, border, prior_diag, coupling_block)

        def bypass_elimination():
            return (jnp.zeros_like(coupling_block), jnp.zeros((covars, mesh_width), coupling_block.dtype), jnp.zeros((covars, covars), coupling_block.dtype))
        schur_update, lateral_block, apex_schur_block = lax.cond(local_length == 2, perform_elimination, bypass_elimination)
        has_left = partition_position > 0
        fill = jnp.where(has_left, jnp.where(local_length == 2, schur_update, coupling_block), 0.0)
        left_update = jnp.where(has_left, schur_update, 0.0)
        left_side = jnp.where(has_left, lateral_block, 0.0)
        own_sep = hessian[0] + prior_diag + schur_update
        own_border = border[0] + lateral_block
        return (own_sep, own_border, fill, left_update, left_side, tip_data + apex_schur_block)
    own_sep, own_border, fill, left_update, left_side, tip_parts = lax.map(one_part, jnp.arange(N_TM, dtype=jnp.int32))
    shifted_update = jnp.concatenate([left_update[1:], jnp.zeros_like(left_update[:1])], axis=0)
    shifted_side = jnp.concatenate([left_side[1:], jnp.zeros_like(left_side[:1])], axis=0)
    sep_block = own_sep + shifted_update
    sep_border = own_border + shifted_side
    tip = jnp.sum(tip_parts, axis=0) + tau_fixed * jnp.eye(covars, dtype=jnp.float32)
    return (sep_block, fill, sep_border, tip)
```

```python
import functools

import jax
import jax.numpy as jnp
from jax import lax
from jax.experimental import pallas as pl
from jax.experimental.pallas import tpu as pltpu
from jax.sharding import PartitionSpec as P

HIGHEST = lax.Precision.HIGHEST
BF = jnp.bfloat16
F32 = jnp.float32
PAD = 128
TILE = 128
ASSUMED = 0.3
CLOSE = 0.7
SMALL = 0.006 * 0.006


def nn(a, b):
    return lax.dot_general(a, b, (((1,), (0,)), ((), ())), preferred_element_type=F32)


def nt(a, b):
    return lax.dot_general(a, b, (((1,), (1,)), ((), ())), preferred_element_type=F32)


def nt3(ah, al, bh, bl):
    return nt(ah, bh) + nt(ah, bl) + nt(al, bh)


def split(x):
    hi = x.astype(BF)
    return hi, (x - hi.astype(F32)).astype(BF)


def eye_part(rows, cols, col_lo):
    r = lax.broadcasted_iota(jnp.int32, (rows, cols), 0)
    c = lax.broadcasted_iota(jnp.int32, (rows, cols), 1) + col_lo
    return jnp.where(r == c, 1.0, 0.0).astype(F32)


def next_bound(a):
    q = a * (2.0 - a)
    return 2.0 / (1.0 + q), 2.0 * q / (1.0 + q)


def partition_kernel(
    chunk, nblk, hyper_ref, meta_ref, prec_ref, recs_ref,
    sep_ref, fill_ref, packed_ref, border_ref, lateral_ref, tip_ref,
    sh, sl, h1, b1, ah, al, x, res, rth, rtl, yt, rest, wt, a32, x32, t32,
):
    m = prec_ref.shape[0]
    covars = border_ref.shape[0]
    rho, tau = hyper_ref[0], hyper_ref[1]
    c_diag = (1.0 + rho * rho) * tau
    c_off = -rho * tau
    my_end, length, position = meta_ref[0], meta_ref[1], meta_ref[2]
    end_f = my_end.astype(F32)
    two = length == 2

    sep_ref[...] = c_diag * prec_ref[...]
    h1[...] = c_diag * prec_ref[...]
    b1[...] = jnp.zeros_like(b1)
    border_ref[...] = jnp.zeros_like(border_ref)
    tip_ref[...] = jnp.zeros_like(tip_ref)

    def add_chunk(j, _):
        lanes = pl.ds(pl.multiple_of(j * chunk, chunk), chunk)
        slot = end_f - recs_ref[0:1, lanes]
        m0 = jnp.where(slot == 0.0, 1.0, 0.0)
        m1 = jnp.where(slot == 1.0, 1.0, 0.0)
        root = jnp.exp(0.5 * recs_ref[4:5, lanes])
        ids = [recs_ref[u : u + 1, lanes] for u in (1, 2, 3)]
        vals = [recs_ref[u : u + 1, lanes] * root for u in (5, 6, 7)]

        def build(i, _):
            rows = pl.ds(pl.multiple_of(i * 64, 64), 64)
            node = (lax.broadcasted_iota(jnp.int32, (64, chunk), 0) + i * 64).astype(F32)
            s = jnp.where(node == ids[0], vals[0], 0.0)
            s = s + jnp.where(node == ids[1], vals[1], 0.0)
            s = s + jnp.where(node == ids[2], vals[2], 0.0)
            hi, lo = split(s)
            sh[rows, :] = hi
            sl[rows, :] = lo
            return 0

        lax.fori_loop(0, m // 64, build, 0)
        z = recs_ref[8 : 8 + covars, lanes] * root
        z = jnp.concatenate([z, jnp.zeros((PAD - covars, chunk), F32)], axis=0)
        zh, zl = split(z)
        tip_ref[...] += nt3(zh, zl, zh, zl)[:covars, :covars]
        m0h = m0.astype(BF)
        m1h = m1.astype(BF)

        def grow(i, _):
            rows = pl.ds(pl.multiple_of(i * nblk, nblk), nblk)
            bh, bl = sh[rows, :], sl[rows, :]
            bh0, bl0, bh1, bl1 = bh * m0h, bl * m0h, bh * m1h, bl * m1h
            sep_ref[:, rows] += nt3(sh[...], sl[...], bh0, bl0)
            h1[:, rows] += nt3(sh[...], sl[...], bh1, bl1)
            border_ref[:, rows] += nt3(zh, zl, bh0, bl0)[:covars]
            b1[:, rows] += nt3(zh, zl, bh1, bl1)
            return 0

        lax.fori_loop(0, m // nblk, grow, 0)
        return 0

    lax.fori_loop(0, recs_ref.shape[1] // chunk, add_chunk, 0)

    picked = eye_part(m, m, 0) * h1[...]
    d_row = lax.rsqrt(jnp.sum(picked, axis=0, keepdims=True))
    d_col = lax.rsqrt(jnp.sum(picked, axis=1, keepdims=True))
    scaled = h1[...] * d_row * d_col
    a32[...] = scaled
    hi, lo = split(scaled)
    ah[...] = hi
    al[...] = lo
    top = jnp.max(jnp.sum(jnp.abs(scaled), axis=0, keepdims=True))
    hi, lo = split(c_off * prec_ref[...] * d_row)
    rth[0:m, :] = hi
    rtl[0:m, :] = lo
    hi, lo = split(b1[...] * d_row)
    rth[m : m + PAD, :] = hi
    rtl[m : m + PAD, :] = lo

    a0 = jnp.float32(ASSUMED)
    alpha = (2.0 - a0) / top
    s0, a1 = next_bound(a0)
    x[0] = (s0 * alpha * (2.0 * eye_part(m, m, 0) - alpha * scaled)).astype(BF)

    def newton(state):
        k, a, _, cur = state
        s, later = next_bound(a)

        def residual(i, total):
            cols = pl.ds(pl.multiple_of(i * nblk, nblk), nblk)
            r = eye_part(m, nblk, i * nblk) - nn(ah[...], x[cur, :, cols])
            res[:, cols] = r.astype(BF)
            return jnp.maximum(total, jnp.sum(jnp.abs(r), axis=0, keepdims=True))

        total = jnp.max(lax.fori_loop(0, m // nblk, residual, jnp.zeros((1, nblk), F32)))

        def improve(i, _):
            cols = pl.ds(pl.multiple_of(i * nblk, nblk), nblk)
            old = x[cur, :, cols].astype(F32)
            x[1 - cur, :, cols] = (s * (old + nn(x[cur], res[:, cols]))).astype(BF)
            return 0

        lax.fori_loop(0, m // nblk, improve, 0)
        return k + 1, later, total, 1 - cur

    _, _, total, cur = lax.while_loop(
        lambda st: jnp.logical_and(st[0] < 10, st[2] > CLOSE),
        newton,
        (jnp.int32(0), a1, jnp.float32(1e9), jnp.int32(0)),
    )

    def first(i, _):
        cols = pl.ds(pl.multiple_of(i * nblk, nblk), nblk)
        yt[:, cols] = nn(rth[...], x[cur, :, cols]).astype(BF)
        return 0

    def second(i, sums):
        cols = pl.ds(pl.multiple_of(i * nblk, nblk), nblk)
        right = rth[:, cols].astype(F32)
        r = right - nn(yt[...], ah[:, cols])
        r = r + (rtl[:, cols].astype(F32) - nn(yt[...], al[:, cols]))
        rest[:, cols] = r.astype(BF)
        left_sum, right_sum = sums
        return (
            left_sum + jnp.sum(r * r, axis=0, keepdims=True),
            right_sum + jnp.sum(right * right, axis=0, keepdims=True),
        )

    steps = m // nblk
    lax.fori_loop(0, steps, first, 0)
    zero = jnp.zeros((1, nblk), F32)
    left_sum, right_sum = lax.fori_loop(0, steps, second, (zero, zero))
    good = jnp.logical_and(total <= CLOSE, jnp.sum(left_sum) <= SMALL * jnp.sum(right_sum))

    def put_result(cols_lo, width, col):
        cols = pl.ds(cols_lo, width)
        u = jnp.where(two, -col[:m], 0.0)
        sep_ref[:, cols] += u
        fill_ref[:, cols] = jnp.where(
            position == 0, 0.0, jnp.where(two, u, c_off * prec_ref[:, cols])
        )
        side = jnp.where(two, -col[m : m + covars], 0.0)
        border_ref[:, cols] += side
        lateral_ref[:, cols] = side

    def put_tip(block):
        tip_ref[...] += jnp.where(two, -block[:covars, :covars], 0.0)

    @pl.when(good)
    def _():
        def third(i, _):
            cols = pl.ds(pl.multiple_of(i * nblk, nblk), nblk)
            w = yt[:, cols].astype(F32) + nn(rest[...], x[cur, :, cols])
            wt[:, cols] = w.astype(BF)
            return 0

        def last(i, _):
            lo = pl.multiple_of(i * nblk, nblk)
            rows = pl.ds(lo, nblk)
            col = nt(rth[...], yt[rows, :]) + nt(rtl[...], yt[rows, :]) + nt(wt[...], rest[rows, :])
            put_result(lo, nblk, col)
            return 0

        lax.fori_loop(0, steps, third, 0)
        lax.fori_loop(0, steps, last, 0)
        tail = pl.ds(m, PAD)
        put_tip(
            nt(rth[tail, :], yt[tail, :])
            + nt(rtl[tail, :], yt[tail, :])
            + nt(wt[tail, :], rest[tail, :])
        )

    @pl.when(jnp.logical_not(good))
    def _():
        blk = TILE
        bands = m // blk
        all_rows = m + PAD

        def exact(a, b):
            return lax.dot_general(
                a, b, (((1,), (0,)), ((), ())), precision=HIGHEST, preferred_element_type=F32
            )

        x32[0] = alpha * eye_part(m, m, 0)

        def step(state):
            k, a, _, cur = state
            s, later = next_bound(a)

            def residual(i, total):
                cols = pl.ds(pl.multiple_of(i * blk, blk), blk)
                r = eye_part(m, blk, i * blk) - exact(a32[...], x32[cur, :, cols])
                t32[0:m, cols] = r
                return total + jnp.sum(r * r)

            total = lax.fori_loop(0, bands, residual, jnp.float32(0.0))

            def improve(i, _):
                cols = pl.ds(pl.multiple_of(i * blk, blk), blk)
                x32[1 - cur, :, cols] = s * (
                    x32[cur, :, cols] + exact(x32[cur], t32[0:m, cols])
                )
                return 0

            lax.fori_loop(0, bands, improve, 0)
            return k + 1, later, total, 1 - cur

        _, _, _, cur32 = lax.while_loop(
            lambda st: jnp.logical_and(st[0] < 40, st[2] > 1e-3),
            step,
            (jnp.int32(0), a0, jnp.float32(1e9), jnp.int32(0)),
        )
        inv = x32.at[cur32]

        def right(lo):
            return rth[pl.ds(lo, blk), :].astype(F32) + rtl[pl.ds(lo, blk), :].astype(F32)

        def solve(i, _):
            lo = pl.multiple_of(i * blk, blk)
            r = right(lo)
            y = exact(r, inv[...])
            for _ in range(2):
                y = y + exact(r - exact(y, a32[...]), inv[...])
            t32[pl.ds(lo, blk), :] = y
            return 0

        lax.fori_loop(0, all_rows // blk, solve, 0)

        def exact_nt(a, b):
            return lax.dot_general(
                a, b, (((1,), (1,)), ((), ())), precision=HIGHEST, preferred_element_type=F32
            )

        whole = rth[...].astype(F32) + rtl[...].astype(F32)

        def last(i, _):
            lo = pl.multiple_of(i * blk, blk)
            put_result(lo, blk, exact_nt(whole, t32[pl.ds(lo, blk), :]))
            return 0

        lax.fori_loop(0, bands, last, 0)
        put_tip(exact_nt(right(m), t32[pl.ds(m, PAD), :]))

    at = 0
    for r in range(m // TILE):
        for c in range(r + 1):
            packed_ref[at * TILE : (at + 1) * TILE, :] = fill_ref[
                r * TILE : (r + 1) * TILE, c * TILE : (c + 1) * TILE
            ]
            at += 1


def add_kernel(meta_ref, own_ref, packed_ref, border_ref, side_ref, sep_ref, out_border_ref):
    m = own_ref.shape[0]
    take = meta_ref[3] == 2
    at = 0
    for r in range(m // TILE):
        for c in range(r + 1):
            block = jnp.where(take, packed_ref[at * TILE : (at + 1) * TILE, :], 0.0)
            rs, cs = slice(r * TILE, (r + 1) * TILE), slice(c * TILE, (c + 1) * TILE)
            sep_ref[rs, cs] = own_ref[rs, cs] + block
            if r != c:
                sep_ref[cs, rs] = own_ref[cs, rs] + block.T
            at += 1
    out_border_ref[...] = border_ref[...] + jnp.where(take, side_ref[...], 0.0)


def local(hyper, spatial_prec, part_lengths, reading_index, reading_value, reading_cov):
    m = spatial_prec.shape[0]
    covars = reading_cov.shape[0]
    tm = lax.axis_size("tm")
    reads = reading_index.shape[2]
    cap = reads // tm
    position = lax.axis_index("tm")
    fields = 8 + covars
    packed = jnp.concatenate(
        [reading_index[:, 0].astype(F32), reading_value[:, 0], reading_cov[:, 0]], axis=0
    )
    packed = packed.reshape(fields, tm, cap).transpose(1, 0, 2)
    packed = lax.all_to_all(packed, "tm", split_axis=0, concat_axis=0, tiled=True)
    recs = packed.transpose(1, 0, 2).reshape(fields, reads)

    upto = jnp.arange(tm, dtype=jnp.int32)
    my_end = jnp.sum(jnp.where(upto <= position, part_lengths, 0)) - 1
    my_len = jnp.sum(jnp.where(upto == position, part_lengths, 0))
    next_len = jnp.sum(jnp.where(upto == position + 1, part_lengths, 0))
    meta = jnp.stack([my_end, my_len, position, next_len]).astype(jnp.int32)

    chunk = min(reads, 1024)
    nblk = 256 if m % 256 == 0 else 128
    tiles = m // TILE
    packed_rows = tiles * (tiles + 1) // 2 * TILE
    vmem = pl.BlockSpec(memory_space=pltpu.VMEM)
    smem = pl.BlockSpec(memory_space=pltpu.SMEM)
    shape = lambda *s: jax.ShapeDtypeStruct(s, F32)
    own, fill, lower, border, lateral, tip = pl.pallas_call(
        functools.partial(partition_kernel, chunk, nblk),
        out_shape=(
            shape(m, m), shape(m, m), shape(packed_rows, TILE),
            shape(covars, m), shape(covars, m), shape(covars, covars),
        ),
        in_specs=[smem, smem, vmem, vmem],
        out_specs=[vmem] * 6,
        scratch_shapes=[
            pltpu.VMEM((m, chunk), BF),
            pltpu.VMEM((m, chunk), BF),
            pltpu.VMEM((m, m), F32),
            pltpu.VMEM((PAD, m), F32),
            pltpu.VMEM((m, m), BF),
            pltpu.VMEM((m, m), BF),
            pltpu.VMEM((2, m, m), BF),
            pltpu.VMEM((m, m), BF),
            pltpu.VMEM((m + PAD, m), BF),
            pltpu.VMEM((m + PAD, m), BF),
            pltpu.VMEM((m + PAD, m), BF),
            pltpu.VMEM((m + PAD, m), BF),
            pltpu.VMEM((m + PAD, m), BF),
            pltpu.VMEM((m, m), F32),
            pltpu.VMEM((2, m, m), F32),
            pltpu.VMEM((m + PAD, m), F32),
        ],
        compiler_params=pltpu.CompilerParams(vmem_limit_bytes=60 * 1024 * 1024),
        name="partition",
    )(hyper, meta, spatial_prec, recs)

    back = [(i + 1, i) for i in range(tm - 1)]
    from_right = lax.ppermute(lower, "tm", back)
    side_right = lax.ppermute(lateral, "tm", back)
    tip = lax.psum(tip, "tm") + hyper[2] * jnp.eye(covars, dtype=F32)
    sep, sep_border = pl.pallas_call(
        add_kernel,
        out_shape=(shape(m, m), shape(covars, m)),
        in_specs=[smem, vmem, vmem, vmem, vmem],
        out_specs=[vmem] * 2,
        compiler_params=pltpu.CompilerParams(vmem_limit_bytes=32 * 1024 * 1024),
        name="add_right",
    )(meta, own, from_right, border, side_right)
    return (sep[None], fill[None], sep_border[None], tip)


def solution(mesh):
    in_specs = (
        P("groups"),
        P(),
        P("groups"),
        P(None, ("groups", "tm"), None),
        P(None, ("groups", "tm"), None),
        P(None, ("groups", "tm"), None),
    )
    out_specs = (
        P(("groups", "tm"), None, None),
        P(("groups", "tm"), None, None),
        P(("groups", "tm"), None, None),
        P("groups", None),
    )
    return jax.shard_map(local, mesh=mesh, in_specs=in_specs, out_specs=out_specs, check_vma=False)
```

```python
import functools

import jax
import jax.numpy as jnp
from jax import lax
from jax.experimental import pallas as pl
from jax.experimental.pallas import tpu as pltpu
from jax.sharding import PartitionSpec as P

HIGHEST = lax.Precision.HIGHEST
MESH = pl.DeviceIdType.MESH
BF = jnp.bfloat16
F32 = jnp.float32
PAD = 128
TILE = 128
ASSUMED = 0.3
CLOSE = 0.7
SMALL = 0.006 * 0.006


def nn(a, b):
    return lax.dot_general(a, b, (((1,), (0,)), ((), ())), preferred_element_type=F32)


def nt(a, b):
    return lax.dot_general(a, b, (((1,), (1,)), ((), ())), preferred_element_type=F32)


def nt3(ah, al, bh, bl):
    return nt(ah, bh) + nt(ah, bl) + nt(al, bh)


def split(x):
    hi = x.astype(BF)
    return hi, (x - hi.astype(F32)).astype(BF)


def eye_part(rows, cols, col_lo):
    r = lax.broadcasted_iota(jnp.int32, (rows, cols), 0)
    c = lax.broadcasted_iota(jnp.int32, (rows, cols), 1) + col_lo
    return jnp.where(r == c, 1.0, 0.0).astype(F32)


def next_bound(a):
    q = a * (2.0 - a)
    return 2.0 / (1.0 + q), 2.0 * q / (1.0 + q)


def greet(tm):
    me = lax.axis_index("tm")
    barrier = pltpu.get_barrier_semaphore()

    def signal(i, _):
        pl.semaphore_signal(
            barrier, inc=1, device_id={"tm": lax.rem(me + i, tm)}, device_id_type=MESH
        )
        return 0

    lax.fori_loop(1, tm, signal, 0)
    pl.semaphore_wait(barrier, tm - 1)
    return me


def to_all(tm, me, source, slots, send_sem, recv_sem):
    def start(i, _):
        to = lax.rem(me + i, tm)
        pltpu.make_async_remote_copy(
            src_ref=source(to), dst_ref=slots.at[me], send_sem=send_sem.at[to],
            recv_sem=recv_sem.at[me], device_id={"tm": to}, device_id_type=MESH,
        ).start()
        return 0

    def finish(i, _):
        to = lax.rem(me + i, tm)
        copy = pltpu.make_async_remote_copy(
            src_ref=source(to), dst_ref=slots.at[to], send_sem=send_sem.at[to],
            recv_sem=recv_sem.at[to], device_id={"tm": to}, device_id_type=MESH,
        )
        copy.wait_send()
        copy.wait_recv()
        return 0

    lax.fori_loop(1, tm, start, 0)
    lax.fori_loop(1, tm, finish, 0)


def readings_kernel(
    tm, index_ref, value_ref, cov_ref, out_ref, stage, outgoing, slots, send_sem, recv_sem
):
    cap = outgoing.shape[2]
    stage[0:4, :] = index_ref[:, 0, :].astype(F32)
    stage[4:8, :] = value_ref[:, 0, :]
    stage[8:, :] = cov_ref[:, 0, :]
    for p in range(tm):
        outgoing[p] = stage[:, p * cap : (p + 1) * cap]
    me = greet(tm)
    slots[me] = outgoing[me]
    to_all(tm, me, lambda p: outgoing.at[p], slots, send_sem, recv_sem)
    for p in range(tm):
        out_ref[:, p * cap : (p + 1) * cap] = slots[p]


def tip_kernel(tm, hyper_ref, mine_ref, out_ref, slots, send_sem, recv_sem):
    rows, cols = mine_ref.shape
    me = greet(tm)
    slots[me] = mine_ref[...]
    to_all(tm, me, lambda p: mine_ref, slots, send_sem, recv_sem)
    total = hyper_ref[2] * eye_part(rows, cols, 0)
    total = lax.fori_loop(0, tm, lambda p, t: t + slots[p], total)
    out_ref[...] = total[:, : out_ref.shape[1]]


def day_sums(chunk, nblk, wanted, end_f, recs_ref, covars, sh, sl, hess_ref, border_ref, tip_ref):
    m = hess_ref.shape[0]

    def add_chunk(j, _):
        lanes = pl.ds(pl.multiple_of(j * chunk, chunk), chunk)
        slot = end_f - recs_ref[0:1, lanes]
        keep = jnp.where(slot == wanted, 1.0, 0.0).astype(BF)
        root = jnp.exp(0.5 * recs_ref[4:5, lanes])
        ids = [recs_ref[u : u + 1, lanes] for u in (1, 2, 3)]
        vals = [recs_ref[u : u + 1, lanes] * root for u in (5, 6, 7)]

        def build(i, _):
            rows = pl.ds(pl.multiple_of(i * 64, 64), 64)
            node = (lax.broadcasted_iota(jnp.int32, (64, chunk), 0) + i * 64).astype(F32)
            s = jnp.where(node == ids[0], vals[0], 0.0)
            s = s + jnp.where(node == ids[1], vals[1], 0.0)
            s = s + jnp.where(node == ids[2], vals[2], 0.0)
            hi, lo = split(s)
            sh[rows, :] = hi
            sl[rows, :] = lo
            return 0

        lax.fori_loop(0, m // 64, build, 0)
        z = recs_ref[8 : 8 + covars, lanes] * root
        z = jnp.concatenate([z, jnp.zeros((PAD - covars, chunk), F32)], axis=0)
        zh, zl = split(z)
        if tip_ref is not None:
            tip_ref[...] += nt3(zh, zl, zh, zl)[:covars]

        def grow(i, _):
            rows = pl.ds(pl.multiple_of(i * nblk, nblk), nblk)
            bh, bl = sh[rows, :] * keep, sl[rows, :] * keep
            hess_ref[:, rows] += nt3(sh[...], sl[...], bh, bl)
            border_ref[:, rows] += nt3(zh, zl, bh, bl)[: border_ref.shape[0]]
            return 0

        lax.fori_loop(0, m // nblk, grow, 0)
        return 0

    lax.fori_loop(0, recs_ref.shape[1] // chunk, add_chunk, 0)


def last_day(lens_ref):
    me = lax.axis_index("tm")
    return me, lax.fori_loop(0, me + 1, lambda p, t: t + lens_ref[p], jnp.int32(-1))


def separator_kernel(
    chunk, nblk, hyper_ref, lens_ref, prec_ref, recs_ref, after_ref, sep_ref, border_ref, sh, sl
):
    del after_ref
    rho, tau = hyper_ref[0], hyper_ref[1]
    _, my_end = last_day(lens_ref)
    sep_ref[...] = (1.0 + rho * rho) * tau * prec_ref[...]
    border_ref[...] = jnp.zeros_like(border_ref)
    covars = border_ref.shape[0]
    day_sums(
        chunk, nblk, 0.0, my_end.astype(F32), recs_ref, covars, sh, sl, sep_ref, border_ref, None
    )


def partition_kernel(
    chunk, nblk, covars, hyper_ref, lens_ref, prec_ref, recs_ref,
    fill_ref, packed_ref, tip_ref,
    sh, sl, h1, b1, ah, al, x, res, rth, rtl, yt, rest, wt, a32, x32, t32,
):
    m = prec_ref.shape[0]
    rho, tau = hyper_ref[0], hyper_ref[1]
    c_diag = (1.0 + rho * rho) * tau
    c_off = -rho * tau
    position, my_end = last_day(lens_ref)
    two = lens_ref[position] == 2

    h1[...] = c_diag * prec_ref[...]
    b1[...] = jnp.zeros_like(b1)
    tip_ref[...] = jnp.zeros_like(tip_ref)
    day_sums(
        chunk, nblk, 1.0, my_end.astype(F32), recs_ref, covars, sh, sl, h1, b1, tip_ref
    )

    picked = eye_part(m, m, 0) * h1[...]
    d_row = lax.rsqrt(jnp.sum(picked, axis=0, keepdims=True))
    d_col = lax.rsqrt(jnp.sum(picked, axis=1, keepdims=True))
    scaled = h1[...] * d_row * d_col
    a32[...] = scaled
    hi, lo = split(scaled)
    ah[...] = hi
    al[...] = lo
    top = jnp.max(jnp.sum(jnp.abs(scaled), axis=0, keepdims=True))
    hi, lo = split(c_off * prec_ref[...] * d_row)
    rth[0:m, :] = hi
    rtl[0:m, :] = lo
    hi, lo = split(b1[...] * d_row)
    rth[m : m + PAD, :] = hi
    rtl[m : m + PAD, :] = lo

    a0 = jnp.float32(ASSUMED)
    alpha = (2.0 - a0) / top
    s0, a1 = next_bound(a0)
    x[0] = (s0 * alpha * (2.0 * eye_part(m, m, 0) - alpha * scaled)).astype(BF)

    def newton(state):
        k, a, _, cur = state
        s, later = next_bound(a)

        def residual(i, total):
            cols = pl.ds(pl.multiple_of(i * nblk, nblk), nblk)
            r = eye_part(m, nblk, i * nblk) - nn(ah[...], x[cur, :, cols])
            res[:, cols] = r.astype(BF)
            return jnp.maximum(total, jnp.sum(jnp.abs(r), axis=0, keepdims=True))

        total = jnp.max(lax.fori_loop(0, m // nblk, residual, jnp.zeros((1, nblk), F32)))

        def improve(i, _):
            cols = pl.ds(pl.multiple_of(i * nblk, nblk), nblk)
            old = x[cur, :, cols].astype(F32)
            x[1 - cur, :, cols] = (s * (old + nn(x[cur], res[:, cols]))).astype(BF)
            return 0

        lax.fori_loop(0, m // nblk, improve, 0)
        return k + 1, later, total, 1 - cur

    _, _, total, cur = lax.while_loop(
        lambda st: jnp.logical_and(st[0] < 10, st[2] > CLOSE),
        newton,
        (jnp.int32(0), a1, jnp.float32(1e9), jnp.int32(0)),
    )

    def first(i, _):
        cols = pl.ds(pl.multiple_of(i * nblk, nblk), nblk)
        yt[:, cols] = nn(rth[...], x[cur, :, cols]).astype(BF)
        return 0

    def second(i, sums):
        cols = pl.ds(pl.multiple_of(i * nblk, nblk), nblk)
        right = rth[:, cols].astype(F32)
        r = right - nn(yt[...], ah[:, cols])
        r = r + (rtl[:, cols].astype(F32) - nn(yt[...], al[:, cols]))
        rest[:, cols] = r.astype(BF)
        left_sum, right_sum = sums
        return (
            left_sum + jnp.sum(r * r, axis=0, keepdims=True),
            right_sum + jnp.sum(right * right, axis=0, keepdims=True),
        )

    steps = m // nblk
    lax.fori_loop(0, steps, first, 0)
    zero = jnp.zeros((1, nblk), F32)
    left_sum, right_sum = lax.fori_loop(0, steps, second, (zero, zero))
    good = jnp.logical_and(total <= CLOSE, jnp.sum(left_sum) <= SMALL * jnp.sum(right_sum))

    def put_result(cols_lo, width, col):
        cols = pl.ds(cols_lo, width)
        u = jnp.where(two, -col[:m], 0.0)
        h1[:, cols] = u
        fill_ref[:, cols] = jnp.where(
            position == 0, 0.0, jnp.where(two, u, c_off * prec_ref[:, cols])
        )
        b1[0:covars, cols] = jnp.where(two, -col[m : m + covars], 0.0)

    def put_tip(block):
        tip_ref[...] += jnp.where(two, -block[:covars], 0.0)

    @pl.when(good)
    def _():
        def third(i, _):
            cols = pl.ds(pl.multiple_of(i * nblk, nblk), nblk)
            w = yt[:, cols].astype(F32) + nn(rest[...], x[cur, :, cols])
            wt[:, cols] = w.astype(BF)
            return 0

        def last(i, _):
            lo = pl.multiple_of(i * nblk, nblk)
            rows = pl.ds(lo, nblk)
            col = nt(rth[...], yt[rows, :]) + nt(rtl[...], yt[rows, :]) + nt(wt[...], rest[rows, :])
            put_result(lo, nblk, col)
            return 0

        lax.fori_loop(0, steps, third, 0)
        lax.fori_loop(0, steps, last, 0)
        tail = pl.ds(m, PAD)
        put_tip(
            nt(rth[tail, :], yt[tail, :])
            + nt(rtl[tail, :], yt[tail, :])
            + nt(wt[tail, :], rest[tail, :])
        )

    @pl.when(jnp.logical_not(good))
    def _():
        blk = TILE
        bands = m // blk
        all_rows = m + PAD

        def exact(a, b):
            return lax.dot_general(
                a, b, (((1,), (0,)), ((), ())), precision=HIGHEST, preferred_element_type=F32
            )

        x32[0] = alpha * eye_part(m, m, 0)

        def step(state):
            k, a, _, cur = state
            s, later = next_bound(a)

            def residual(i, total):
                cols = pl.ds(pl.multiple_of(i * blk, blk), blk)
                r = eye_part(m, blk, i * blk) - exact(a32[...], x32[cur, :, cols])
                t32[0:m, cols] = r
                return total + jnp.sum(r * r)

            total = lax.fori_loop(0, bands, residual, jnp.float32(0.0))

            def improve(i, _):
                cols = pl.ds(pl.multiple_of(i * blk, blk), blk)
                x32[1 - cur, :, cols] = s * (
                    x32[cur, :, cols] + exact(x32[cur], t32[0:m, cols])
                )
                return 0

            lax.fori_loop(0, bands, improve, 0)
            return k + 1, later, total, 1 - cur

        _, _, _, cur32 = lax.while_loop(
            lambda st: jnp.logical_and(st[0] < 40, st[2] > 1e-3),
            step,
            (jnp.int32(0), a0, jnp.float32(1e9), jnp.int32(0)),
        )
        inv = x32.at[cur32]

        def right(lo):
            return rth[pl.ds(lo, blk), :].astype(F32) + rtl[pl.ds(lo, blk), :].astype(F32)

        def solve(i, _):
            lo = pl.multiple_of(i * blk, blk)
            r = right(lo)
            y = exact(r, inv[...])
            for _ in range(2):
                y = y + exact(r - exact(y, a32[...]), inv[...])
            t32[pl.ds(lo, blk), :] = y
            return 0

        lax.fori_loop(0, all_rows // blk, solve, 0)

        def exact_nt(a, b):
            return lax.dot_general(
                a, b, (((1,), (1,)), ((), ())), precision=HIGHEST, preferred_element_type=F32
            )

        whole = rth[...].astype(F32) + rtl[...].astype(F32)

        def last(i, _):
            lo = pl.multiple_of(i * blk, blk)
            put_result(lo, blk, exact_nt(whole, t32[pl.ds(lo, blk), :]))
            return 0

        lax.fori_loop(0, bands, last, 0)
        put_tip(exact_nt(right(m), t32[pl.ds(m, PAD), :]))

    at = 0
    for r in range(m // TILE):
        for c in range(r + 1):
            packed_ref[at * TILE : (at + 1) * TILE, :] = h1[
                r * TILE : (r + 1) * TILE, c * TILE : (c + 1) * TILE
            ]
            at += 1
    for r in range(m // TILE):
        lo = at * TILE + r * covars
        packed_ref[lo : lo + covars, :] = b1[0:covars, r * TILE : (r + 1) * TILE]


def add_kernel(own_ref, mine_ref, right_ref, border_ref, sep_ref, out_border_ref):
    m = own_ref.shape[0]
    covars = border_ref.shape[0]
    at = 0
    for r in range(m // TILE):
        for c in range(r + 1):
            rows = slice(at * TILE, (at + 1) * TILE)
            block = mine_ref[rows, :] + right_ref[rows, :]
            rs, cs = slice(r * TILE, (r + 1) * TILE), slice(c * TILE, (c + 1) * TILE)
            sep_ref[rs, cs] = own_ref[rs, cs] + block
            if r != c:
                sep_ref[cs, rs] = own_ref[cs, rs] + block.T
            at += 1
    for r in range(m // TILE):
        rows = slice(at * TILE + r * covars, at * TILE + (r + 1) * covars)
        cs = slice(r * TILE, (r + 1) * TILE)
        out_border_ref[:, cs] = border_ref[:, cs] + (mine_ref[rows, :] + right_ref[rows, :])


def local(hyper, spatial_prec, part_lengths, reading_index, reading_value, reading_cov):
    m = spatial_prec.shape[0]
    covars = reading_cov.shape[0]
    tm = lax.axis_size("tm")
    reads = reading_index.shape[2]
    cap = reads // tm
    fields = 8 + covars
    chunk = min(reads, 1024)
    nblk = 256 if m % 256 == 0 else 128
    tiles = m // TILE
    packed_rows = tiles * (tiles + 1) // 2 * TILE + tiles * covars
    vmem = pl.BlockSpec(memory_space=pltpu.VMEM)
    smem = pl.BlockSpec(memory_space=pltpu.SMEM)
    shape = lambda *s: jax.ShapeDtypeStruct(s, F32)
    dma = pltpu.SemaphoreType.DMA

    recs = pl.pallas_call(
        functools.partial(readings_kernel, tm),
        out_shape=shape(fields, reads),
        in_specs=[vmem] * 3,
        out_specs=vmem,
        scratch_shapes=[
            pltpu.VMEM((fields, reads), F32),
            pltpu.VMEM((tm, fields, cap), F32),
            pltpu.VMEM((tm, fields, cap), F32),
            dma((tm,)),
            dma((tm,)),
        ],
        compiler_params=pltpu.CompilerParams(
            collective_id=0, has_side_effects=True, vmem_limit_bytes=32 * 1024 * 1024
        ),
        name="readings",
    )(reading_index, reading_value, reading_cov)

    fill, packed, tip = pl.pallas_call(
        functools.partial(partition_kernel, chunk, nblk, covars),
        out_shape=(shape(m, m), shape(packed_rows, TILE), shape(covars, PAD)),
        in_specs=[smem, smem, vmem, vmem],
        out_specs=[vmem] * 3,
        scratch_shapes=[
            pltpu.VMEM((m, chunk), BF),
            pltpu.VMEM((m, chunk), BF),
            pltpu.VMEM((m, m), F32),
            pltpu.VMEM((PAD, m), F32),
            pltpu.VMEM((m, m), BF),
            pltpu.VMEM((m, m), BF),
            pltpu.VMEM((2, m, m), BF),
            pltpu.VMEM((m, m), BF),
            pltpu.VMEM((m + PAD, m), BF),
            pltpu.VMEM((m + PAD, m), BF),
            pltpu.VMEM((m + PAD, m), BF),
            pltpu.VMEM((m + PAD, m), BF),
            pltpu.VMEM((m + PAD, m), BF),
            pltpu.VMEM((m, m), F32),
            pltpu.VMEM((2, m, m), F32),
            pltpu.VMEM((m + PAD, m), F32),
        ],
        compiler_params=pltpu.CompilerParams(vmem_limit_bytes=58 * 1024 * 1024),
        name="partition",
    )(hyper, part_lengths, spatial_prec, recs)

    from_right = lax.ppermute(packed, "tm", [(i + 1, i) for i in range(tm - 1)])
    own, border = pl.pallas_call(
        functools.partial(separator_kernel, chunk, nblk),
        out_shape=(shape(m, m), shape(covars, m)),
        in_specs=[smem, smem, vmem, vmem, vmem],
        out_specs=[vmem] * 2,
        scratch_shapes=[pltpu.VMEM((m, chunk), BF), pltpu.VMEM((m, chunk), BF)],
        compiler_params=pltpu.CompilerParams(vmem_limit_bytes=40 * 1024 * 1024),
        cost_estimate=pl.CostEstimate(
            flops=6 * m * m * reads, bytes_accessed=8 * m * m, transcendentals=0
        ),
        name="separator",
    )(hyper, part_lengths, spatial_prec, recs, tip)
    tip = pl.pallas_call(
        functools.partial(tip_kernel, tm),
        out_shape=shape(covars, covars),
        in_specs=[smem, vmem],
        out_specs=vmem,
        scratch_shapes=[pltpu.VMEM((tm, covars, PAD), F32), dma((tm,)), dma((tm,))],
        compiler_params=pltpu.CompilerParams(
            collective_id=1, has_side_effects=True, vmem_limit_bytes=32 * 1024 * 1024
        ),
        name="tip_sum",
    )(hyper, tip)
    sep, sep_border = pl.pallas_call(
        add_kernel,
        out_shape=(shape(m, m), shape(covars, m)),
        in_specs=[vmem] * 4,
        out_specs=[vmem] * 2,
        compiler_params=pltpu.CompilerParams(vmem_limit_bytes=32 * 1024 * 1024),
        name="add_right",
    )(own, packed, from_right, border)
    return (sep[None], fill[None], sep_border[None], tip)


def solution(mesh):
    in_specs = (
        P("groups"),
        P(),
        P("groups"),
        P(None, ("groups", "tm"), None),
        P(None, ("groups", "tm"), None),
        P(None, ("groups", "tm"), None),
    )
    out_specs = (
        P(("groups", "tm"), None, None),
        P(("groups", "tm"), None, None),
        P(("groups", "tm"), None, None),
        P("groups", None),
    )
    return jax.shard_map(local, mesh=mesh, in_specs=in_specs, out_specs=out_specs, check_vma=False)
```

```python
import functools

import jax
import jax.numpy as jnp
from jax import lax
from jax.experimental import pallas as pl
from jax.experimental.pallas import tpu as pltpu
from jax.sharding import PartitionSpec as P

HIGHEST = lax.Precision.HIGHEST
MESH = pl.DeviceIdType.MESH
BF = jnp.bfloat16
F32 = jnp.float32
PAD = 128
TILE = 128
ASSUMED = 0.3
CLOSE = 0.7
SMALL = 0.006 * 0.006


def nn(a, b):
    return lax.dot_general(a, b, (((1,), (0,)), ((), ())), preferred_element_type=F32)


def nt(a, b):
    return lax.dot_general(a, b, (((1,), (1,)), ((), ())), preferred_element_type=F32)


def nt3(ah, al, bh, bl):
    return nt(ah, bh) + nt(ah, bl) + nt(al, bh)


def split(x):
    hi = x.astype(BF)
    return hi, (x - hi.astype(F32)).astype(BF)


def eye_part(rows, cols, col_lo):
    r = lax.broadcasted_iota(jnp.int32, (rows, cols), 0)
    c = lax.broadcasted_iota(jnp.int32, (rows, cols), 1) + col_lo
    return jnp.where(r == c, 1.0, 0.0).astype(F32)


def next_bound(a):
    q = a * (2.0 - a)
    return 2.0 / (1.0 + q), 2.0 * q / (1.0 + q)


def greet(tm):
    me = lax.axis_index("tm")
    barrier = pltpu.get_barrier_semaphore()

    def signal(i, _):
        pl.semaphore_signal(
            barrier, inc=1, device_id={"tm": lax.rem(me + i, tm)}, device_id_type=MESH
        )
        return 0

    lax.fori_loop(1, tm, signal, 0)
    pl.semaphore_wait(barrier, tm - 1)
    return me


def to_all(tm, me, source, slots, send_sem, recv_sem):
    def start(i, _):
        to = lax.rem(me + i, tm)
        pltpu.make_async_remote_copy(
            src_ref=source(to), dst_ref=slots.at[me], send_sem=send_sem.at[to],
            recv_sem=recv_sem.at[me], device_id={"tm": to}, device_id_type=MESH,
        ).start()
        return 0

    def finish(i, _):
        to = lax.rem(me + i, tm)
        copy = pltpu.make_async_remote_copy(
            src_ref=source(to), dst_ref=slots.at[to], send_sem=send_sem.at[to],
            recv_sem=recv_sem.at[to], device_id={"tm": to}, device_id_type=MESH,
        )
        copy.wait_send()
        copy.wait_recv()
        return 0

    lax.fori_loop(1, tm, start, 0)
    lax.fori_loop(1, tm, finish, 0)


def readings_kernel(
    tm, index_ref, value_ref, cov_ref, out_ref, stage, outgoing, slots, send_sem, recv_sem
):
    cap = outgoing.shape[2]
    stage[0:4, :] = index_ref[:, 0, :].astype(F32)
    stage[4:8, :] = value_ref[:, 0, :]
    stage[8:, :] = cov_ref[:, 0, :]
    for p in range(tm):
        outgoing[p] = stage[:, p * cap : (p + 1) * cap]
    me = greet(tm)
    slots[me] = outgoing[me]
    to_all(tm, me, lambda p: outgoing.at[p], slots, send_sem, recv_sem)
    for p in range(tm):
        out_ref[:, p * cap : (p + 1) * cap] = slots[p]


def tip_kernel(tm, hyper_ref, mine_ref, after_ref, out_ref, slots, send_sem, recv_sem):
    del after_ref
    rows, cols = mine_ref.shape
    me = greet(tm)
    slots[me] = mine_ref[...]
    to_all(tm, me, lambda p: mine_ref, slots, send_sem, recv_sem)
    total = hyper_ref[2] * eye_part(rows, cols, 0)
    total = lax.fori_loop(0, tm, lambda p, t: t + slots[p], total)
    out_ref[...] = total[:, : out_ref.shape[1]]


def day_sums(chunk, nblk, wanted, end_f, recs_ref, covars, sh, sl, hess_ref, border_ref, tip_ref):
    m = hess_ref.shape[0]

    def add_chunk(j, _):
        lanes = pl.ds(pl.multiple_of(j * chunk, chunk), chunk)
        slot = end_f - recs_ref[0:1, lanes]
        keep = jnp.where(slot == wanted, 1.0, 0.0).astype(BF)
        root = jnp.exp(0.5 * recs_ref[4:5, lanes])
        ids = [recs_ref[u : u + 1, lanes] for u in (1, 2, 3)]
        vals = [recs_ref[u : u + 1, lanes] * root for u in (5, 6, 7)]

        def build(i, _):
            rows = pl.ds(pl.multiple_of(i * 64, 64), 64)
            node = (lax.broadcasted_iota(jnp.int32, (64, chunk), 0) + i * 64).astype(F32)
            s = jnp.where(node == ids[0], vals[0], 0.0)
            s = s + jnp.where(node == ids[1], vals[1], 0.0)
            s = s + jnp.where(node == ids[2], vals[2], 0.0)
            hi, lo = split(s)
            sh[rows, :] = hi
            sl[rows, :] = lo
            return 0

        lax.fori_loop(0, m // 64, build, 0)
        z = recs_ref[8 : 8 + covars, lanes] * root
        z = jnp.concatenate([z, jnp.zeros((PAD - covars, chunk), F32)], axis=0)
        zh, zl = split(z)
        sh[m : m + PAD, :] = zh
        sl[m : m + PAD, :] = zl
        if tip_ref is not None:
            tip_ref[...] += nt3(zh, zl, zh, zl)[:covars]

        def grow(i, _):
            rows = pl.ds(pl.multiple_of(i * nblk, nblk), nblk)
            bh, bl = sh[rows, :] * keep, sl[rows, :] * keep
            both = nt3(sh[...], sl[...], bh, bl)
            hess_ref[:, rows] += both[:m]
            border_ref[:, rows] += both[m : m + border_ref.shape[0]]
            return 0

        lax.fori_loop(0, m // nblk, grow, 0)
        return 0

    lax.fori_loop(0, recs_ref.shape[1] // chunk, add_chunk, 0)


def last_day(lens_ref):
    me = lax.axis_index("tm")
    return me, lax.fori_loop(0, me + 1, lambda p, t: t + lens_ref[p], jnp.int32(-1))


def separator_kernel(
    chunk, nblk, hyper_ref, lens_ref, prec_ref, recs_ref, after_ref, sep_ref, border_ref, sh, sl
):
    del after_ref
    rho, tau = hyper_ref[0], hyper_ref[1]
    _, my_end = last_day(lens_ref)
    sep_ref[...] = (1.0 + rho * rho) * tau * prec_ref[...]
    border_ref[...] = jnp.zeros_like(border_ref)
    covars = border_ref.shape[0]
    day_sums(
        chunk, nblk, 0.0, my_end.astype(F32), recs_ref, covars, sh, sl, sep_ref, border_ref, None
    )


def partition_kernel(
    chunk, nblk, covars, hyper_ref, lens_ref, prec_ref, recs_ref,
    fill_ref, packed_ref, tip_ref,
    sh, sl, h1, b1, ah, al, x, res, rth, rtl, yt, rest, wt, a32, x32, t32,
):
    m = prec_ref.shape[0]
    rho, tau = hyper_ref[0], hyper_ref[1]
    c_diag = (1.0 + rho * rho) * tau
    c_off = -rho * tau
    position, my_end = last_day(lens_ref)
    two = lens_ref[position] == 2

    h1[...] = c_diag * prec_ref[...]
    b1[...] = jnp.zeros_like(b1)
    tip_ref[...] = jnp.zeros_like(tip_ref)
    day_sums(
        chunk, nblk, 1.0, my_end.astype(F32), recs_ref, covars, sh, sl, h1, b1, tip_ref
    )

    picked = eye_part(m, m, 0) * h1[...]
    d_row = lax.rsqrt(jnp.sum(picked, axis=0, keepdims=True))
    d_col = lax.rsqrt(jnp.sum(picked, axis=1, keepdims=True))
    scaled = h1[...] * d_row * d_col
    a32[...] = scaled
    hi, lo = split(scaled)
    ah[...] = hi
    al[...] = lo
    top = jnp.max(jnp.sum(jnp.abs(scaled), axis=0, keepdims=True))
    hi, lo = split(c_off * prec_ref[...] * d_row)
    rth[0:m, :] = hi
    rtl[0:m, :] = lo
    hi, lo = split(b1[...] * d_row)
    rth[m : m + PAD, :] = hi
    rtl[m : m + PAD, :] = lo

    a0 = jnp.float32(ASSUMED)
    alpha = (2.0 - a0) / top
    s0, a1 = next_bound(a0)
    x[0] = (s0 * alpha * (2.0 * eye_part(m, m, 0) - alpha * scaled)).astype(BF)

    def newton(state):
        k, a, _, cur = state
        s, later = next_bound(a)

        def residual(i, total):
            cols = pl.ds(pl.multiple_of(i * nblk, nblk), nblk)
            r = eye_part(m, nblk, i * nblk) - nn(ah[...], x[cur, :, cols])
            res[:, cols] = r.astype(BF)
            return jnp.maximum(total, jnp.sum(jnp.abs(r), axis=0, keepdims=True))

        total = jnp.max(lax.fori_loop(0, m // nblk, residual, jnp.zeros((1, nblk), F32)))

        def improve(i, _):
            cols = pl.ds(pl.multiple_of(i * nblk, nblk), nblk)
            old = x[cur, :, cols].astype(F32)
            x[1 - cur, :, cols] = (s * (old + nn(x[cur], res[:, cols]))).astype(BF)
            return 0

        lax.fori_loop(0, m // nblk, improve, 0)
        return k + 1, later, total, 1 - cur

    _, _, total, cur = lax.while_loop(
        lambda st: jnp.logical_and(st[0] < 10, st[2] > CLOSE),
        newton,
        (jnp.int32(0), a1, jnp.float32(1e9), jnp.int32(0)),
    )

    def first(i, _):
        cols = pl.ds(pl.multiple_of(i * nblk, nblk), nblk)
        yt[:, cols] = nn(rth[...], x[cur, :, cols]).astype(BF)
        return 0

    def second(i, sums):
        cols = pl.ds(pl.multiple_of(i * nblk, nblk), nblk)
        right = rth[:, cols].astype(F32)
        r = right - nn(yt[...], ah[:, cols])
        r = r + (rtl[:, cols].astype(F32) - nn(yt[...], al[:, cols]))
        rest[:, cols] = r.astype(BF)
        left_sum, right_sum = sums
        return (
            left_sum + jnp.sum(r * r, axis=0, keepdims=True),
            right_sum + jnp.sum(right * right, axis=0, keepdims=True),
        )

    steps = m // nblk
    lax.fori_loop(0, steps, first, 0)
    zero = jnp.zeros((1, nblk), F32)
    left_sum, right_sum = lax.fori_loop(0, steps, second, (zero, zero))
    good = jnp.logical_and(total <= CLOSE, jnp.sum(left_sum) <= SMALL * jnp.sum(right_sum))

    def put_result(cols_lo, width, col):
        cols = pl.ds(cols_lo, width)
        u = jnp.where(two, -col[:m], 0.0)
        h1[:, cols] = u
        fill_ref[:, cols] = jnp.where(
            position == 0, 0.0, jnp.where(two, u, c_off * prec_ref[:, cols])
        )
        b1[0:covars, cols] = jnp.where(two, -col[m : m + covars], 0.0)

    def put_tip(block):
        tip_ref[...] += jnp.where(two, -block[:covars], 0.0)

    @pl.when(good)
    def _():
        def third(i, _):
            cols = pl.ds(pl.multiple_of(i * nblk, nblk), nblk)
            w = yt[:, cols].astype(F32) + nn(rest[...], x[cur, :, cols])
            wt[:, cols] = w.astype(BF)
            return 0

        def last(i, _):
            lo = pl.multiple_of(i * nblk, nblk)
            rows = pl.ds(lo, nblk)
            col = nt(rth[...], yt[rows, :]) + nt(rtl[...], yt[rows, :]) + nt(wt[...], rest[rows, :])
            put_result(lo, nblk, col)
            return 0

        lax.fori_loop(0, steps, third, 0)
        lax.fori_loop(0, steps, last, 0)
        tail = pl.ds(m, PAD)
        put_tip(
            nt(rth[tail, :], yt[tail, :])
            + nt(rtl[tail, :], yt[tail, :])
            + nt(wt[tail, :], rest[tail, :])
        )

    @pl.when(jnp.logical_not(good))
    def _():
        blk = TILE
        bands = m // blk
        all_rows = m + PAD

        def exact(a, b):
            return lax.dot_general(
                a, b, (((1,), (0,)), ((), ())), precision=HIGHEST, preferred_element_type=F32
            )

        x32[0] = alpha * eye_part(m, m, 0)

        def step(state):
            k, a, _, cur = state
            s, later = next_bound(a)

            def residual(i, total):
                cols = pl.ds(pl.multiple_of(i * blk, blk), blk)
                r = eye_part(m, blk, i * blk) - exact(a32[...], x32[cur, :, cols])
                t32[0:m, cols] = r
                return total + jnp.sum(r * r)

            total = lax.fori_loop(0, bands, residual, jnp.float32(0.0))

            def improve(i, _):
                cols = pl.ds(pl.multiple_of(i * blk, blk), blk)
                x32[1 - cur, :, cols] = s * (
                    x32[cur, :, cols] + exact(x32[cur], t32[0:m, cols])
                )
                return 0

            lax.fori_loop(0, bands, improve, 0)
            return k + 1, later, total, 1 - cur

        _, _, _, cur32 = lax.while_loop(
            lambda st: jnp.logical_and(st[0] < 40, st[2] > 1e-3),
            step,
            (jnp.int32(0), a0, jnp.float32(1e9), jnp.int32(0)),
        )
        inv = x32.at[cur32]

        def right(lo):
            return rth[pl.ds(lo, blk), :].astype(F32) + rtl[pl.ds(lo, blk), :].astype(F32)

        def solve(i, _):
            lo = pl.multiple_of(i * blk, blk)
            r = right(lo)
            y = exact(r, inv[...])
            for _ in range(2):
                y = y + exact(r - exact(y, a32[...]), inv[...])
            t32[pl.ds(lo, blk), :] = y
            return 0

        lax.fori_loop(0, all_rows // blk, solve, 0)

        def exact_nt(a, b):
            return lax.dot_general(
                a, b, (((1,), (1,)), ((), ())), precision=HIGHEST, preferred_element_type=F32
            )

        whole = rth[...].astype(F32) + rtl[...].astype(F32)

        def last(i, _):
            lo = pl.multiple_of(i * blk, blk)
            put_result(lo, blk, exact_nt(whole, t32[pl.ds(lo, blk), :]))
            return 0

        lax.fori_loop(0, bands, last, 0)
        put_tip(exact_nt(right(m), t32[pl.ds(m, PAD), :]))

    at = 0
    for r in range(m // TILE):
        for c in range(r + 1):
            packed_ref[at * TILE : (at + 1) * TILE, :] = h1[
                r * TILE : (r + 1) * TILE, c * TILE : (c + 1) * TILE
            ]
            at += 1
    for r in range(m // TILE):
        lo = at * TILE + r * covars
        packed_ref[lo : lo + covars, :] = b1[0:covars, r * TILE : (r + 1) * TILE]


def add_kernel(own_ref, mine_ref, right_ref, border_ref, sep_ref, out_border_ref):
    m = own_ref.shape[0]
    covars = border_ref.shape[0]
    at = 0
    for r in range(m // TILE):
        for c in range(r + 1):
            rows = slice(at * TILE, (at + 1) * TILE)
            block = mine_ref[rows, :] + right_ref[rows, :]
            rs, cs = slice(r * TILE, (r + 1) * TILE), slice(c * TILE, (c + 1) * TILE)
            sep_ref[rs, cs] = own_ref[rs, cs] + block
            if r != c:
                sep_ref[cs, rs] = own_ref[cs, rs] + block.T
            at += 1
    for r in range(m // TILE):
        rows = slice(at * TILE + r * covars, at * TILE + (r + 1) * covars)
        cs = slice(r * TILE, (r + 1) * TILE)
        out_border_ref[:, cs] = border_ref[:, cs] + (mine_ref[rows, :] + right_ref[rows, :])


def local(hyper, spatial_prec, part_lengths, reading_index, reading_value, reading_cov):
    m = spatial_prec.shape[0]
    covars = reading_cov.shape[0]
    tm = lax.axis_size("tm")
    reads = reading_index.shape[2]
    cap = reads // tm
    fields = 8 + covars
    chunk = min(reads, 1024)
    nblk = 256 if m % 256 == 0 else 128
    tiles = m // TILE
    packed_rows = tiles * (tiles + 1) // 2 * TILE + tiles * covars
    vmem = pl.BlockSpec(memory_space=pltpu.VMEM)
    smem = pl.BlockSpec(memory_space=pltpu.SMEM)
    anywhere = pl.BlockSpec(memory_space=pl.ANY)
    shape = lambda *s: jax.ShapeDtypeStruct(s, F32)
    dma = pltpu.SemaphoreType.DMA

    recs = pl.pallas_call(
        functools.partial(readings_kernel, tm),
        out_shape=shape(fields, reads),
        in_specs=[vmem] * 3,
        out_specs=vmem,
        scratch_shapes=[
            pltpu.VMEM((fields, reads), F32),
            pltpu.VMEM((tm, fields, cap), F32),
            pltpu.VMEM((tm, fields, cap), F32),
            dma((tm,)),
            dma((tm,)),
        ],
        compiler_params=pltpu.CompilerParams(
            collective_id=0, has_side_effects=True, vmem_limit_bytes=32 * 1024 * 1024
        ),
        name="readings",
    )(reading_index, reading_value, reading_cov)

    fill, packed, tip = pl.pallas_call(
        functools.partial(partition_kernel, chunk, nblk, covars),
        out_shape=(shape(m, m), shape(packed_rows, TILE), shape(covars, PAD)),
        in_specs=[smem, smem, vmem, vmem],
        out_specs=[vmem] * 3,
        scratch_shapes=[
            pltpu.VMEM((m + PAD, chunk), BF),
            pltpu.VMEM((m + PAD, chunk), BF),
            pltpu.VMEM((m, m), F32),
            pltpu.VMEM((PAD, m), F32),
            pltpu.VMEM((m, m), BF),
            pltpu.VMEM((m, m), BF),
            pltpu.VMEM((2, m, m), BF),
            pltpu.VMEM((m, m), BF),
            pltpu.VMEM((m + PAD, m), BF),
            pltpu.VMEM((m + PAD, m), BF),
            pltpu.VMEM((m + PAD, m), BF),
            pltpu.VMEM((m + PAD, m), BF),
            pltpu.VMEM((m + PAD, m), BF),
            pltpu.VMEM((m, m), F32),
            pltpu.VMEM((2, m, m), F32),
            pltpu.VMEM((m + PAD, m), F32),
        ],
        compiler_params=pltpu.CompilerParams(vmem_limit_bytes=58 * 1024 * 1024),
        name="partition",
    )(hyper, part_lengths, spatial_prec, recs)

    from_right = lax.ppermute(packed, "tm", [(i + 1, i) for i in range(tm - 1)])
    own, border = pl.pallas_call(
        functools.partial(separator_kernel, chunk, nblk),
        out_shape=(shape(m, m), shape(covars, m)),
        in_specs=[smem, smem, vmem, vmem, anywhere],
        out_specs=[vmem] * 2,
        scratch_shapes=[pltpu.VMEM((m + PAD, chunk), BF)] * 2,
        compiler_params=pltpu.CompilerParams(vmem_limit_bytes=40 * 1024 * 1024),
        cost_estimate=pl.CostEstimate(
            flops=6 * m * m * reads, bytes_accessed=8 * m * m, transcendentals=0
        ),
        name="separator",
    )(hyper, part_lengths, spatial_prec, recs, tip)
    tip = pl.pallas_call(
        functools.partial(tip_kernel, tm),
        out_shape=shape(covars, covars),
        in_specs=[smem, vmem, anywhere],
        out_specs=vmem,
        scratch_shapes=[pltpu.VMEM((tm, covars, PAD), F32), dma((tm,)), dma((tm,))],
        compiler_params=pltpu.CompilerParams(
            collective_id=1, has_side_effects=True, vmem_limit_bytes=32 * 1024 * 1024
        ),
        name="tip_sum",
    )(hyper, tip, border)
    sep, sep_border = pl.pallas_call(
        add_kernel,
        out_shape=(shape(m, m), shape(covars, m)),
        in_specs=[vmem] * 4,
        out_specs=[vmem] * 2,
        compiler_params=pltpu.CompilerParams(vmem_limit_bytes=32 * 1024 * 1024),
        name="add_right",
    )(own, packed, from_right, border)
    return (sep[None], fill[None], sep_border[None], tip)


def solution(mesh):
    in_specs = (
        P("groups"),
        P(),
        P("groups"),
        P(None, ("groups", "tm"), None),
        P(None, ("groups", "tm"), None),
        P(None, ("groups", "tm"), None),
    )
    out_specs = (
        P(("groups", "tm"), None, None),
        P(("groups", "tm"), None, None),
        P(("groups", "tm"), None, None),
        P("groups", None),
    )
    return jax.shard_map(local, mesh=mesh, in_specs=in_specs, out_specs=out_specs, check_vma=False)
```
